32 devices in a mesh: group: 4 (over x, core), fsdp: 8 (over z, y).
Axes of the slice: x: 2, y: 2, z: 4, core: 2. Of those that a mesh axis runs over, the one named last changes fastest.
Arguments:
- hidden: bfloat16 [32, 128, 8192], P('group', None, 'fsdp'), may hold values from -6 to 6
- norm_gain: bfloat16 [8192], replicated, may hold values from 0.099609375 to 1.8984375
- w_query: bfloat16 [8192, 8192], P('group', 'fsdp'), may hold values from -0.0625 to 0.0625
- key_projection_weight: bfloat16 [8192, 1024], P('group'), may hold values from -0.0625 to 0.0625
- value_projection_weight: bfloat16 [8192, 1024], P('group'), may hold values from -0.0625 to 0.0625
- prompt_key_cache: bfloat16 [2048, 1024], P('group'), may hold values from -74 to 74
- prompt_value_cache: bfloat16 [2048, 1024], P('group'), may hold values from -6 to 6
- keep_flag: int32 [32], replicated, may hold values from 0 to 1, as said below
- destination: int32 [32], replicated, may hold values from 0 to 15, as said below
- row_counts: int32 [32], replicated, may hold values from 32 to 128
Outputs:
- attended: bfloat16 [16, 128, 8192], P('group', None, 'fsdp')
The draws below stay inside these ranges and needn't reach their ends.
Inputs may be any that keep to these rules, and one draw needn't show every extreme that they name: `keep_flag`: exactly 16 blocks are kept. `destination`: the kept blocks name the slots 0 to 15, each exactly once. Among the 8 blocks g * 8 to g * 8 + 7, the kept ones that name a slot of d * 4 to d * 4 + 3 number either 0 or exactly 1. Entries of dropped blocks are arbitrary slot numbers.
All inputs are finite; a program needn't handle non-finite values.
Results may differ from the reference program's by a relative error of at most 0.012.
The reference program's roundings to bfloat16 on the way count: a program that leaves them out, or rounds other values in their place, can miss the bound.
Values may be sent and summed in bfloat16 or wider, within the bound.
A program may use at most 192 MiB of HBM per device.

```python
import jax
import jax.numpy as jnp
from jax import lax

MODEL_WIDTH = 8192
QUERY_HEADS = 64
KEY_VALUE_HEADS = 8
HEAD_SIZE = 128
BLOCK_TOKENS = 128
PROMPT_TOKENS = 2048
IN_DEV = 8
CAP = 1
OUT_DEV = 4
BLOCKS = 32
SLOTS = 16


def route_plan(key):
    group_total = BLOCKS // IN_DEV
    pick_keys = jax.random.split(key, 4)
    pool_copies = min(IN_DEV // CAP, group_total)
    pick_pool = jnp.tile(jnp.arange(group_total, dtype=jnp.int32), pool_copies)
    pick_pool = jax.random.permutation(pick_keys[0], pick_pool)
    chosen = jnp.sort(pick_pool[:group_total * (OUT_DEV // CAP)])
    pick_index = jnp.arange(chosen.shape[0], dtype=jnp.int32)
    dest_order = jax.random.permutation(pick_keys[1], group_total).astype(jnp.int32)
    target_dev = dest_order[pick_index % group_total]
    slot_base = pick_index // group_total * CAP
    earlier = (chosen[None, :] == chosen[:, None]) & (pick_index[None, :] < pick_index[:, None])
    pick_rank = jnp.sum(earlier.astype(jnp.int32), axis=1)
    slot_perm = jax.vmap(lambda sub_key: jax.random.permutation(sub_key, IN_DEV))(jax.random.split(pick_keys[2], group_total)).astype(jnp.int32)
    keep_flags = jnp.zeros((BLOCKS,), jnp.int32)
    dest_slots = jax.random.randint(pick_keys[3], (BLOCKS,), 0, OUT_DEV * group_total, dtype=jnp.int32)
    for copy_index in range(CAP):
        block_ids = chosen * IN_DEV + slot_perm[chosen, pick_rank * CAP + copy_index]
        keep_flags = keep_flags.at[block_ids].set(1)
        dest_slots = dest_slots.at[block_ids].set(target_dev * OUT_DEV + slot_base + copy_index)
    return (keep_flags, dest_slots)


def draw_keep_flag(key, part):
    return route_plan(key)[0]


def draw_destination(key, part):
    return route_plan(key)[1]


def draw_prompt_key_cache(key, part):
    key = jax.random.fold_in(key, 7)
    jitter_random_key, position_random_key, polarity_random_key, permute_random_key = jax.random.split(key, 4)
    random_jitter = jnp.clip(jax.random.normal(jitter_random_key, (PROMPT_TOKENS, KEY_VALUE_HEADS, HEAD_SIZE), jnp.float32), -6.0, 6.0)
    lower_limit = 30.0
    upper_limit = 64.0
    head_permuted_order = jax.random.permutation(permute_random_key, KEY_VALUE_HEADS).astype(jnp.float32)
    jitter_scale = lower_limit * (upper_limit / lower_limit) ** (head_permuted_order / (KEY_VALUE_HEADS - 1))
    token_positions = jax.random.permutation(position_random_key, PROMPT_TOKENS)[:2 * KEY_VALUE_HEADS].astype(jnp.int32).reshape(KEY_VALUE_HEADS, 2)
    rows = jnp.arange(PROMPT_TOKENS, dtype=jnp.int32)
    planted = jnp.any(rows[:, None, None] == token_positions[None, :, :], axis=2).astype(jnp.float32)
    sign_flips = (2 * jax.random.randint(polarity_random_key, (KEY_VALUE_HEADS, HEAD_SIZE), 0, 2) - 1).astype(jnp.float32)
    joined_keys = random_jitter + planted[:, :, None] * jitter_scale[None, :, None] * sign_flips[None, :, :]
    return joined_keys.reshape(PROMPT_TOKENS, KEY_VALUE_HEADS * HEAD_SIZE).astype(jnp.bfloat16)


def touch_ends(entries, stream_key, smallest, largest):
    longest = entries.shape.index(max(entries.shape))
    spots = []
    for shift in (0, 1):
        where = [jax.random.randint(jax.random.fold_in(stream_key, axis), (), 0, length) for axis, length in enumerate(entries.shape)]
        where[longest] = (where[longest] + shift) % entries.shape[longest]
        spots.append(tuple(where))
    return entries.at[spots[0]].set(smallest).at[spots[1]].set(largest)


def block_levels(key, dims, cuts, least, high):
    loudness, own = 1.0, jax.random.fold_in(key, 6)
    for dim, parts in cuts:
        heights = jnp.exp(jax.random.uniform(jax.random.fold_in(own, dim), (parts,), jnp.float32, least / len(cuts), high / len(cuts)))
        loudness = loudness * jnp.repeat(heights, dims[dim] // parts).reshape([-1 if axis == dim else 1 for axis in range(len(dims))])
    return loudness


def noise(rng, dims, spread, reach, cuts=(), held_as=jnp.bfloat16):
    drawn = jax.random.normal(rng, dims, jnp.float32) * spread
    if len(cuts) > 0:
        drawn = block_levels(rng, dims, cuts, -0.22, 0.18) * drawn
    return jnp.clip(drawn, min=-reach, max=reach).astype(held_as)


def setup_inputs(seed: int = 0) -> dict:
    keys = jax.random.split(jax.random.key(seed), 11)
    return {
        "hidden": noise(keys[0], (BLOCKS, BLOCK_TOKENS, MODEL_WIDTH), 1.0, 6.0, ((0, 4), (2, 8))),
        "norm_gain": jnp.clip(1.0 + 0.18 * jax.random.normal(keys[1], (MODEL_WIDTH,), jnp.float32), 0.099609375, 1.8984375).astype(jnp.bfloat16),
        "w_query": noise(keys[2], (MODEL_WIDTH, QUERY_HEADS * HEAD_SIZE), MODEL_WIDTH ** -0.5, 0.0625, ((0, 4), (1, 8))),
        "key_projection_weight": noise(keys[3], (MODEL_WIDTH, KEY_VALUE_HEADS * HEAD_SIZE), MODEL_WIDTH ** -0.5, 0.0625, ((0, 4),)),
        "value_projection_weight": noise(keys[4], (MODEL_WIDTH, KEY_VALUE_HEADS * HEAD_SIZE), MODEL_WIDTH ** -0.5, 0.0625, ((0, 4),)),
        "prompt_key_cache": draw_prompt_key_cache(jax.random.fold_in(keys[10], 71), 0),
        "prompt_value_cache": noise(keys[6], (PROMPT_TOKENS, KEY_VALUE_HEADS * HEAD_SIZE), 1.0, 6.0, ((0, 4),)),
        "keep_flag": draw_keep_flag(jax.random.fold_in(keys[10], 71), 0),
        "destination": draw_destination(jax.random.fold_in(keys[10], 71), 0),
        "row_counts": touch_ends(jax.random.randint(keys[9], (BLOCKS,), BLOCK_TOKENS // 4, BLOCK_TOKENS + 1), jax.random.fold_in(keys[9], 1), BLOCK_TOKENS // 4, BLOCK_TOKENS).astype(jnp.int32),
    }


EPSILON = 1e-05
ROPE_THETA = 500000.0
CONTEXT_BASE = 8192.0
STRETCH = 8.0
MASKED_SCORE = -1e+30

def rope_tables(length, offset):
    half_dim = HEAD_SIZE // 2
    base_rate = ROPE_THETA ** (-(jnp.arange(half_dim, dtype=jnp.float32) * 2.0 / HEAD_SIZE))
    ratio = CONTEXT_BASE * base_rate / (2.0 * jnp.pi)
    smooth = jnp.clip((ratio - 1.0) / 3.0, 0.0, 1.0)
    inverse_rate = (1.0 - smooth) * base_rate / STRETCH + smooth * base_rate
    token_positions = jnp.arange(length, dtype=jnp.float32) + offset
    angles = token_positions[:, None] * inverse_rate[None, :]
    return (jnp.cos(angles), jnp.sin(angles))

def rotate(values, cosine, sine_table):
    half_dim = values.shape[-1] // 2
    first_half = values[..., :half_dim]
    second = values[..., half_dim:]
    cosine = cosine[:, None, :]
    sine_table = sine_table[:, None, :]
    return jnp.concatenate([first_half * cosine - second * sine_table, second * cosine + first_half * sine_table], axis=-1)

def reference(hidden, norm_gain, w_query, key_projection_weight, value_projection_weight, prompt_key_cache, prompt_value_cache, keep_flag, destination, row_counts):
    block_total = keep_flag.shape[0]
    slot_ids = jnp.arange(SLOTS, dtype=jnp.int32)
    matched = (keep_flag[None, :] == 1) & (destination[None, :] == slot_ids[:, None])
    sources = lax.optimization_barrier(jnp.sum(jnp.where(matched, jnp.arange(block_total, dtype=jnp.int32)[None, :], 0), axis=1)).astype(jnp.int32)
    cosine, sine_table = rope_tables(BLOCK_TOKENS, PROMPT_TOKENS)
    query_group_width = QUERY_HEADS // KEY_VALUE_HEADS
    score_scale = HEAD_SIZE ** (-0.5)
    prompt_keys = prompt_key_cache.reshape(PROMPT_TOKENS, KEY_VALUE_HEADS, HEAD_SIZE)
    prompt_values = prompt_value_cache.reshape(PROMPT_TOKENS, KEY_VALUE_HEADS, HEAD_SIZE)
    position = jnp.arange(BLOCK_TOKENS, dtype=jnp.int32)
    columns = jnp.arange(PROMPT_TOKENS + BLOCK_TOKENS, dtype=jnp.int32)
    gain_wide = norm_gain.astype(jnp.float32)

    def one_block(source_block):
        block_rows = hidden[source_block].astype(jnp.float32)
        valid_rows = row_counts[source_block]
        normalized_input = (block_rows * lax.rsqrt(lax.optimization_barrier(jnp.mean(block_rows * block_rows, axis=1, keepdims=True)) + EPSILON) * gain_wide).astype(jnp.bfloat16)
        query_vectors = jnp.dot(normalized_input, w_query, preferred_element_type=jnp.float32).reshape(BLOCK_TOKENS, QUERY_HEADS, HEAD_SIZE)
        fresh_keys = jnp.dot(normalized_input, key_projection_weight, preferred_element_type=jnp.float32).reshape(BLOCK_TOKENS, KEY_VALUE_HEADS, HEAD_SIZE)
        fresh_values = jnp.dot(normalized_input, value_projection_weight, preferred_element_type=jnp.float32).reshape(BLOCK_TOKENS, KEY_VALUE_HEADS, HEAD_SIZE)
        query_vectors = rotate(query_vectors, cosine, sine_table).astype(jnp.bfloat16)
        fresh_keys = rotate(fresh_keys, cosine, sine_table).astype(jnp.bfloat16)
        fresh_values = fresh_values.astype(jnp.bfloat16)
        all_keys = jnp.concatenate([prompt_keys, fresh_keys], axis=0).astype(jnp.float32)
        all_values = jnp.concatenate([prompt_values, fresh_values], axis=0).astype(jnp.float32)
        grouped_queries = query_vectors.reshape(BLOCK_TOKENS, KEY_VALUE_HEADS, query_group_width, HEAD_SIZE).astype(jnp.float32)
        scores = jnp.einsum('qhgd,khd->qhgk', grouped_queries, all_keys) * score_scale
        own_column = columns[None, :] - PROMPT_TOKENS
        allowed = (columns[None, :] < PROMPT_TOKENS) | (own_column <= position[:, None]) & (own_column < valid_rows)
        scores = jnp.where(allowed[:, None, None, :], scores, MASKED_SCORE)
        row_max = lax.optimization_barrier(jnp.max(scores, axis=3, keepdims=True))
        powers = jnp.exp(scores - row_max)
        row_sum = lax.optimization_barrier(jnp.sum(powers, axis=3))
        weights = lax.optimization_barrier(powers.astype(jnp.bfloat16)).astype(jnp.float32)
        mixed_out = jnp.einsum('qhgk,khd->qhgd', weights, all_values) / row_sum[..., None]
        live_rows = (position < valid_rows)[:, None, None, None]
        return jnp.where(live_rows, mixed_out, 0.0).reshape(BLOCK_TOKENS, QUERY_HEADS * HEAD_SIZE).astype(jnp.bfloat16)
    return lax.map(one_block, sources)
```

```python
import jax
import jax.numpy as jnp
from jax import lax
from jax.sharding import PartitionSpec as P

QUERY_HEADS = 64
KEY_VALUE_HEADS = 8
HEAD_SIZE = 128
PROMPT_TOKENS = 2048
IN_DEV = 8
CAP = 1
OUT_DEV = 4


EPSILON = 1e-05
ROPE_THETA = 500000.0
CONTEXT_BASE = 8192.0
STRETCH = 8.0
MASKED_SCORE = -1e30


def rope_tables(length, offset):
    half_dim = HEAD_SIZE // 2
    base_rate = ROPE_THETA ** (-(jnp.arange(half_dim, dtype=jnp.float32) * 2.0 / HEAD_SIZE))
    ratio = CONTEXT_BASE * base_rate / (2.0 * jnp.pi)
    smooth = jnp.clip((ratio - 1.0) / 3.0, 0.0, 1.0)
    inverse_rate = (1.0 - smooth) * base_rate / STRETCH + smooth * base_rate
    token_positions = jnp.arange(length, dtype=jnp.float32) + offset
    angles = token_positions[:, None] * inverse_rate[None, :]
    return (jnp.cos(angles), jnp.sin(angles))


def rotate(values, cosine, sine_table):
    half_dim = values.shape[-1] // 2
    first_half = values[..., :half_dim]
    second = values[..., half_dim:]
    cosine = cosine[:, None, :]
    sine_table = sine_table[:, None, :]
    return jnp.concatenate(
        [first_half * cosine - second * sine_table, second * cosine + first_half * sine_table],
        axis=-1,
    )


def pack_for_send(values, keep_flag, destination):
    group_count = lax.axis_size("group")
    first = lax.axis_index("group") * IN_DEV
    keep = lax.dynamic_slice_in_dim(keep_flag, first, IN_DEV) == 1
    target = lax.dynamic_slice_in_dim(destination, first, IN_DEV) // OUT_DEV
    peers = jnp.arange(group_count, dtype=jnp.int32)
    chosen = jnp.argmax(keep[None, :] & (target[None, :] == peers[:, None]), axis=1)
    return jnp.stack(
        [lax.dynamic_index_in_dim(values, chosen[d], 0, False) for d in range(group_count)]
    )


def slot_sources(keep_flag, destination):
    slots = lax.axis_index("group") * OUT_DEV + jnp.arange(OUT_DEV, dtype=jnp.int32)
    matched = (keep_flag[None, :] == 1) & (destination[None, :] == slots[:, None])
    return jnp.argmax(matched, axis=1).astype(jnp.int32)


def attend(
    blocks,
    lengths,
    norm_gain,
    w_query,
    key_projection_weight,
    value_projection_weight,
    prompt_key_cache,
    prompt_value_cache,
):
    block_count = blocks.shape[0]
    span_len = blocks.shape[1]
    row_total = block_count * span_len
    gathered = lax.all_gather(blocks, "fsdp", axis=2, tiled=True)
    rows_wide = gathered.reshape(row_total, -1).astype(jnp.float32)
    normalized_input = (
        rows_wide
        * lax.rsqrt(jnp.mean(rows_wide * rows_wide, axis=1, keepdims=True) + EPSILON)
        * norm_gain.astype(jnp.float32)
    ).astype(jnp.bfloat16)
    local_heads = w_query.shape[1] // HEAD_SIZE
    key_value_index = lax.axis_index("fsdp") * local_heads // (QUERY_HEADS // KEY_VALUE_HEADS)
    key_rows = lax.dynamic_slice_in_dim(
        key_projection_weight, key_value_index * HEAD_SIZE, HEAD_SIZE, 1
    )
    value_rows = lax.dynamic_slice_in_dim(
        value_projection_weight, key_value_index * HEAD_SIZE, HEAD_SIZE, 1
    )
    pieces = (
        lax.all_gather(w_query, "group", axis=0, tiled=True),
        lax.all_gather(key_rows, "group", axis=0, tiled=True),
        lax.all_gather(value_rows, "group", axis=0, tiled=True),
    )
    query_vectors = jnp.dot(normalized_input, pieces[0], preferred_element_type=jnp.float32)
    fresh_keys = jnp.dot(normalized_input, pieces[1], preferred_element_type=jnp.float32)
    fresh_values = jnp.dot(normalized_input, pieces[2], preferred_element_type=jnp.float32)
    cosine, sine_table = rope_tables(span_len, PROMPT_TOKENS)
    query_vectors = rotate(
        query_vectors.reshape(block_count, span_len, local_heads, HEAD_SIZE), cosine, sine_table
    ).astype(jnp.bfloat16)
    fresh_keys = (
        rotate(fresh_keys.reshape(block_count, span_len, 1, HEAD_SIZE), cosine, sine_table)
        .reshape(block_count, span_len, HEAD_SIZE)
        .astype(jnp.bfloat16)
    )
    fresh_values = fresh_values.reshape(block_count, span_len, HEAD_SIZE).astype(jnp.bfloat16)
    score_scale = HEAD_SIZE ** (-0.5)
    query_rows = query_vectors.reshape(row_total, local_heads, HEAD_SIZE)
    prompt_keys = lax.dynamic_slice_in_dim(
        prompt_key_cache, key_value_index * HEAD_SIZE, HEAD_SIZE, 1
    )
    prompt_values = lax.dynamic_slice_in_dim(
        prompt_value_cache, key_value_index * HEAD_SIZE, HEAD_SIZE, 1
    )
    pieces = (
        lax.all_gather(prompt_keys, "group", axis=0, tiled=True),
        lax.all_gather(prompt_values, "group", axis=0, tiled=True),
    )
    row_max = jnp.full((row_total, local_heads), MASKED_SCORE, jnp.float32)
    scores = (
        jnp.einsum("rhd,kd->rhk", query_rows, pieces[0], preferred_element_type=jnp.float32)
        * score_scale
    )
    new_max = jnp.maximum(row_max, jnp.max(scores, axis=2))
    powers = jnp.exp(scores - new_max[:, :, None])
    row_sum = jnp.sum(powers, axis=2)
    weighted = jnp.einsum(
        "rhk,kd->rhd", powers.astype(jnp.bfloat16), pieces[1], preferred_element_type=jnp.float32
    )
    row_max, row_sum, weighted = (new_max, row_sum, weighted)
    row_max = row_max.reshape(block_count, span_len, local_heads)
    row_sum = row_sum.reshape(block_count, span_len, local_heads)
    weighted = weighted.reshape(block_count, span_len, local_heads, HEAD_SIZE)
    scores = (
        jnp.einsum("cupy,cly->cupl", query_vectors, fresh_keys, preferred_element_type=jnp.float32)
        * score_scale
    )
    position = jnp.arange(span_len, dtype=jnp.int32)
    allowed = (position[None, None, :] <= position[None, :, None]) & (
        position[None, None, :] < lengths[:, None, None]
    )
    scores = jnp.where(allowed[:, :, None, :], scores, MASKED_SCORE)
    new_max = jnp.maximum(row_max, jnp.max(scores, axis=3))
    powers = jnp.exp(scores - new_max[..., None])
    rescale = jnp.exp(row_max - new_max)
    row_sum = row_sum * rescale + jnp.sum(powers, axis=3)
    weighted = weighted * rescale[..., None] + jnp.einsum(
        "zcmn,znu->zcmu",
        powers.astype(jnp.bfloat16),
        fresh_values,
        preferred_element_type=jnp.float32,
    )
    mixed_out = weighted / row_sum[..., None]
    live_rows = position[None, :] < lengths[:, None]
    mixed_out = jnp.where(live_rows[:, :, None, None], mixed_out, 0.0)
    return mixed_out.reshape(block_count, span_len, local_heads * HEAD_SIZE).astype(jnp.bfloat16)


def body(
    hidden,
    norm_gain,
    w_query,
    key_projection_weight,
    value_projection_weight,
    prompt_key_cache,
    prompt_value_cache,
    keep_flag,
    destination,
    row_counts,
):
    sources = slot_sources(keep_flag, destination)
    packed = pack_for_send(hidden, keep_flag, destination)
    received = lax.all_to_all(packed, "group", split_axis=0, concat_axis=0, tiled=True)
    owners = sources // IN_DEV
    blocks = jnp.stack(
        [lax.dynamic_index_in_dim(received, owners[o], 0, False) for o in range(OUT_DEV)]
    )
    return attend(
        blocks,
        row_counts[sources],
        norm_gain,
        w_query,
        key_projection_weight,
        value_projection_weight,
        prompt_key_cache,
        prompt_value_cache,
    )


def solution(mesh):
    return jax.shard_map(
        body,
        mesh=mesh,
        in_specs=(
            P("group", None, "fsdp"),
            P(),
            P("group", "fsdp"),
            P("group", None),
            P("group", None),
            P("group", None),
            P("group", None),
            P(),
            P(),
            P(),
        ),
        out_specs=P("group", None, "fsdp"),
        check_vma=False,
    )
```

```python
import functools
import math

import jax
import jax.numpy as jnp
from jax import lax
from jax.experimental import pallas as pl
from jax.experimental.pallas import tpu as pltpu
from jax.sharding import PartitionSpec as P

QUERY_HEADS = 64
KEY_VALUE_HEADS = 8
HEAD_SIZE = 128
PROMPT_TOKENS = 2048
IN_DEV = 8
CAP = 1
OUT_DEV = 4


EPSILON = 1e-05
ROPE_THETA = 500000.0
CONTEXT_BASE = 8192.0
STRETCH = 8.0
MASKED_SCORE = -1e30


def rope_tables(length, offset):
    half_dim = HEAD_SIZE // 2
    base_rate = ROPE_THETA ** (-(jnp.arange(half_dim, dtype=jnp.float32) * 2.0 / HEAD_SIZE))
    ratio = CONTEXT_BASE * base_rate / (2.0 * jnp.pi)
    smooth = jnp.clip((ratio - 1.0) / 3.0, 0.0, 1.0)
    inverse_rate = (1.0 - smooth) * base_rate / STRETCH + smooth * base_rate
    token_positions = jnp.arange(length, dtype=jnp.float32) + offset
    angles = token_positions[:, None] * inverse_rate[None, :]
    return (jnp.cos(angles), jnp.sin(angles))


CHUNKS = 4
ROW_TILE = 16
COLUMN_TILE = 2 * HEAD_SIZE
MESH = pl.DeviceIdType.MESH


def project_kernel(
    shape,
    keep_ref,
    dest_ref,
    hidden_ref,
    gain_ref,
    wq_ref,
    wk_ref,
    wv_ref,
    kc_ref,
    vc_ref,
    acc_ref,
    cache_out_ref,
    outbox,
    inbox,
    x_all,
    x_norm,
    w_all,
    cache,
    local_sem,
    inbox_send,
    inbox_recv,
    x_send,
    x_recv,
    w_send,
    w_recv,
):
    groups, shards, lines, width = shape
    columns = shards // lines
    chips = groups // 2
    features = hidden_ref.shape[2]
    span = hidden_ref.shape[1]
    depth = wq_ref.shape[0]
    chunk = depth // CHUNKS
    heads = wq_ref.shape[1] // HEAD_SIZE
    group = lax.axis_index("group")
    shard = lax.axis_index("fsdp")
    chip, core = group // 2, group % 2
    col, line = shard // lines, shard % lines
    head = shard * heads // (QUERY_HEADS // KEY_VALUE_HEADS)
    head_cols = pl.ds(pl.multiple_of(head * HEAD_SIZE, HEAD_SIZE), HEAD_SIZE)

    local = []
    for c in range(CHUNKS):
        rows = pl.ds(c * chunk, chunk)
        mine = w_all.at[group, c]
        copies = [
            pltpu.make_async_copy(
                wq_ref.at[rows, pl.ds(n * HEAD_SIZE, HEAD_SIZE)], mine.at[n], local_sem.at[c, n]
            )
            for n in range(heads)
        ]
        for n, ref in ((heads, wk_ref), (heads + 1, wv_ref)):
            copies.append(
                pltpu.make_async_copy(ref.at[rows, head_cols], mine.at[n], local_sem.at[c, n])
            )
        local.append(copies)
    local.append(
        [
            pltpu.make_async_copy(
                ref.at[:, head_cols], cache.at[group, n], local_sem.at[CHUNKS, n]
            )
            for n, ref in enumerate((kc_ref, vc_ref))
        ]
    )
    for copies in local:
        for copy in copies:
            copy.start()

    x_hops = [
        (col < columns - 1, shard + lines),
        (col > 0, shard - lines),
        (line < lines - 1, shard + 1),
        (line > 0, shard - 1),
    ]
    w_hops = [(chip < chips - 1, group + 2), (chip > 0, group - 2)]
    partner = chip * 2 + 1 - core

    barrier = pltpu.get_barrier_semaphore()
    for j in range(1, groups):
        pl.semaphore_signal(
            barrier, inc=1, device_id={"group": (group + j) % groups}, device_id_type=MESH
        )
    for valid, near in x_hops:

        @pl.when(valid)
        def _(near=near):
            pl.semaphore_signal(barrier, inc=1, device_id={"fsdp": near}, device_id_type=MESH)

    near_count = sum(jnp.where(valid, 1, 0) for valid, _ in x_hops)
    pl.semaphore_wait(barrier, groups - 1 + near_count)

    first = group * IN_DEV

    def chosen(target):
        index = jnp.int32(0)
        for b in range(IN_DEV):
            hit = (keep_ref[first + b] == 1) & (lax.div(dest_ref[first + b], OUT_DEV) == target)
            index = jnp.where(hit, b, index)
        return index

    posts = []
    for j in range(groups - 1, 0, -1):
        peer = (group + j) % groups
        outbox[j - 1] = hidden_ref[chosen(peer)]
        post = pltpu.make_async_remote_copy(
            src_ref=outbox.at[j - 1],
            dst_ref=inbox.at[group],
            send_sem=inbox_send.at[j - 1],
            recv_sem=inbox_recv.at[group],
            device_id={"group": peer},
            device_id_type=MESH,
        )
        post.start()
        posts.append(post)
    inbox[group] = hidden_ref[chosen(group)]

    sends = []

    def x_copy(unit, hop):
        return pltpu.make_async_remote_copy(
            src_ref=x_all.at[unit],
            dst_ref=x_all.at[unit],
            send_sem=x_send.at[unit, hop],
            recv_sem=x_recv.at[unit],
            device_id={"fsdp": x_hops[hop][1]},
            device_id_type=MESH,
        )

    def x_arrival(unit):
        return pltpu.make_async_remote_copy(
            src_ref=x_all.at[unit],
            dst_ref=x_all.at[unit],
            send_sem=x_send.at[unit, 0],
            recv_sem=x_recv.at[unit],
            device_id={"fsdp": (shard + 1) % shards},
            device_id_type=MESH,
        )

    def w_copy(unit, c, hop):
        ref = cache.at[unit] if c == CHUNKS else w_all.at[unit, c]
        return pltpu.make_async_remote_copy(
            src_ref=ref,
            dst_ref=ref,
            send_sem=w_send.at[unit, c, hop],
            recv_sem=w_recv.at[unit, c],
            device_id={"group": partner if hop == 2 else w_hops[hop][1]},
            device_id_type=MESH,
        )

    def launch(copy, when):
        @pl.when(when)
        def _():
            copy.start()

        sends.append((copy, when))

    always = group >= 0
    order = [CHUNKS] + list(range(CHUNKS))
    for c in order:
        for copy in local[c]:
            copy.wait()
        for hop in (0, 1):
            launch(w_copy(group, c, hop), w_hops[hop][0])
        launch(w_copy(group, c, 2), always)

    for j in range(1, groups):
        source = (group + j) % groups
        pltpu.make_async_remote_copy(
            src_ref=inbox.at[source],
            dst_ref=inbox.at[source],
            send_sem=inbox_send.at[j - 1],
            recv_sem=inbox_recv.at[source],
            device_id={"group": source},
            device_id_type=MESH,
        ).wait_recv()
    for o in range(OUT_DEV):
        slot = group * OUT_DEV + o

        def find(b, owner):
            hit = (keep_ref[b] == 1) & (dest_ref[b] == slot)
            return jnp.where(hit, lax.div(b, jnp.int32(IN_DEV)), owner)

        owner = lax.fori_loop(0, groups * IN_DEV, find, jnp.int32(0))
        x_all[shard, pl.ds(o * span, span), :] = inbox[owner]

    for hop in range(4):
        launch(x_copy(shard, hop), x_hops[hop][0])

    def x_column(step):
        for hop, sign in ((0, 1), (1, -1)):
            source = col - sign * step
            there = (source >= 0) & (source < columns)
            unit = source * lines + line

            @pl.when(there)
            def _(unit=unit):
                x_arrival(unit).wait_recv()

            if step < columns - 1:
                launch(x_copy(unit, hop), there & x_hops[hop][0])
            for side in (2, 3):
                launch(x_copy(unit, side), there & x_hops[side][0])

    def x_line(step):
        for hop, sign in ((2, 1), (3, -1)):
            source = line - sign * step
            there = (source >= 0) & (source < lines)
            for k in range(columns):
                unit = k * lines + source

                @pl.when(there)
                def _(unit=unit):
                    x_arrival(unit).wait_recv()

                if step < lines - 1:
                    launch(x_copy(unit, hop), there & x_hops[hop][0])

    def w_chip(step, c):
        for hop, sign in ((0, 1), (1, -1)):
            source = chip - sign * step
            there = (source >= 0) & (source < chips)
            unit = source * 2 + core

            @pl.when(there)
            def _(unit=unit):
                w_copy(unit, c, 2).wait_recv()

            if step < chips - 1:
                launch(w_copy(unit, c, hop), there & w_hops[hop][0])
            launch(w_copy(unit, c, 2), there)

    w_events = [(step, c) for step in range(1, chips) for c in order]
    w_chip(*w_events.pop(0))
    for step in range(1, columns):
        x_column(step)
        if len(w_events) > 2:
            w_chip(*w_events.pop(0))
    for step in range(1, lines):
        x_line(step)

    def normalize(i, carry):
        rows = pl.ds(pl.multiple_of(i * ROW_TILE, ROW_TILE), ROW_TILE)
        total = jnp.zeros((ROW_TILE, features), jnp.float32)
        for f in range(shards):
            values = x_all[f, rows, :].astype(jnp.float32)
            total = total + values * values
        mean = jnp.sum(total, axis=1, keepdims=True) / width
        factor = lax.rsqrt(mean + EPSILON)
        for f in range(shards):
            values = x_all[f, rows, :].astype(jnp.float32)
            x_norm[f, rows, :] = (values * factor * gain_ref[pl.ds(f, 1), :]).astype(jnp.bfloat16)
        return carry

    lax.fori_loop(0, OUT_DEV * span // ROW_TILE, normalize, 0)
    acc_ref[...] = jnp.zeros_like(acc_ref)

    def multiply(unit, c):
        block = unit * (depth // features) + c * chunk // features
        inner = pl.ds(c * chunk % features, chunk)

        def tile(n, carry):
            cols = pl.ds(pl.multiple_of(n * COLUMN_TILE, COLUMN_TILE), COLUMN_TILE)
            acc_ref[:, cols] += jnp.dot(
                x_norm[block, :, inner],
                jnp.concatenate([w_all[unit, c, 2 * n], w_all[unit, c, 2 * n + 1]], axis=1),
                preferred_element_type=jnp.float32,
            )
            return carry

        lax.fori_loop(0, acc_ref.shape[1] // COLUMN_TILE, tile, 0)

    def from_partner(unit, c):
        w_copy(unit, c, 2).wait_recv()

    while w_events:
        w_chip(*w_events.pop(0))
    for d in range(chips):
        for c in order:
            from_partner((chip + d) % chips * 2 + 1 - core, c)
    for unit in range(groups):
        for c in range(CHUNKS):
            multiply(unit, c)
    result = pltpu.make_async_copy(cache, cache_out_ref, local_sem.at[CHUNKS, 2])
    result.start()
    for post in posts:
        post.wait_send()
    for copy, when in sends:

        @pl.when(when)
        def _(copy=copy):
            copy.wait_send()

    result.wait()


def project(shards, groups, hidden, norm_gain, w_query, wk, wv, kc, vc, keep_flag, destination):
    blocks, span, features = hidden.shape
    depth, q_width = w_query.shape
    width = norm_gain.shape[0]
    lines = math.isqrt(shards // 2)
    rows = OUT_DEV * span
    out_width = q_width + 2 * HEAD_SIZE
    cached = kc.shape[0]
    smem = pl.BlockSpec(memory_space=pltpu.SMEM)
    vmem = pl.BlockSpec(memory_space=pltpu.VMEM)
    anywhere = pl.BlockSpec(memory_space=pl.ANY)
    dma = pltpu.SemaphoreType.DMA
    return pl.pallas_call(
        functools.partial(project_kernel, (groups, shards, lines, width)),
        out_shape=(
            jax.ShapeDtypeStruct((rows, out_width), jnp.float32),
            jax.ShapeDtypeStruct((groups, 2, cached, HEAD_SIZE), jnp.bfloat16),
        ),
        in_specs=[smem, smem, vmem, vmem] + [anywhere] * 5,
        out_specs=(vmem, anywhere),
        scratch_shapes=[
            pltpu.VMEM((groups - 1, span, features), jnp.bfloat16),
            pltpu.VMEM((groups, span, features), jnp.bfloat16),
            pltpu.VMEM((shards, rows, features), jnp.bfloat16),
            pltpu.VMEM((shards, rows, features), jnp.bfloat16),
            pltpu.VMEM((groups, CHUNKS, out_width // HEAD_SIZE, depth // CHUNKS, HEAD_SIZE), jnp.bfloat16),
            pltpu.VMEM((groups, 2, cached, HEAD_SIZE), jnp.bfloat16),
            dma((CHUNKS + 1, out_width // HEAD_SIZE)),
            dma((groups - 1,)),
            dma((groups,)),
            dma((shards, 4)),
            dma((shards,)),
            dma((groups, CHUNKS + 1, 3)),
            dma((groups, CHUNKS + 1)),
        ],
        compiler_params=pltpu.CompilerParams(
            collective_id=0, has_side_effects=True, vmem_limit_bytes=58 * 1024 * 1024
        ),
        cost_estimate=pl.CostEstimate(
            flops=2 * rows * width * out_width, bytes_accessed=depth * out_width * 2, transcendentals=0
        ),
        name="gather_and_project",
    )(
        keep_flag,
        destination,
        hidden,
        norm_gain.astype(jnp.float32).reshape(shards, features),
        w_query,
        wk,
        wv,
        kc,
        vc,
    )


def attention_kernel(
    keep_ref, dest_ref, counts_ref, cos_ref, sin_ref, q_ref, k_ref, v_ref, cache_ref, out_ref
):
    slot = lax.axis_index("group") * OUT_DEV + pl.program_id(0)

    def find(b, length):
        hit = (keep_ref[b] == 1) & (dest_ref[b] == slot)
        return jnp.where(hit, counts_ref[b], length)

    length = lax.fori_loop(0, keep_ref.shape[0], find, jnp.int32(0))
    cosine, sine = cos_ref[...], sin_ref[...]

    def turn(values):
        return (values * cosine + pltpu.roll(values, HEAD_SIZE // 2, 1) * sine).astype(jnp.bfloat16)

    span = q_ref.shape[0]
    heads = q_ref.shape[1] // HEAD_SIZE
    queries = jnp.concatenate(
        [turn(q_ref[:, h * HEAD_SIZE : (h + 1) * HEAD_SIZE]) for h in range(heads)], axis=0
    )
    keys = turn(k_ref[...])
    values = v_ref[...].astype(jnp.bfloat16)
    contract = (((1,), (1,)), ((), ()))
    tokens = cache_ref.shape[0] * cache_ref.shape[2]
    prompt_keys = cache_ref[:, 0].reshape(tokens, HEAD_SIZE)
    prompt_values = cache_ref[:, 1].reshape(tokens, HEAD_SIZE)
    cached = lax.dot_general(
        queries, prompt_keys, contract, preferred_element_type=jnp.float32
    )
    fresh = lax.dot_general(queries, keys, contract, preferred_element_type=jnp.float32)
    row = lax.broadcasted_iota(jnp.int32, fresh.shape, 0) % span
    column = lax.broadcasted_iota(jnp.int32, fresh.shape, 1)
    fresh = jnp.where((column <= row) & (column < length), fresh, MASKED_SCORE)
    top = jnp.maximum(
        jnp.max(cached, axis=1, keepdims=True), jnp.max(fresh, axis=1, keepdims=True)
    )
    rate = HEAD_SIZE ** (-0.5) * math.log2(math.e)
    cached = jnp.exp2((cached - top) * rate)
    fresh = jnp.exp2((fresh - top) * rate)
    total = jnp.sum(cached, axis=1, keepdims=True) + jnp.sum(fresh, axis=1, keepdims=True)
    mixed = jnp.dot(
        cached.astype(jnp.bfloat16), prompt_values, preferred_element_type=jnp.float32
    ) + jnp.dot(fresh.astype(jnp.bfloat16), values, preferred_element_type=jnp.float32)
    live = lax.broadcasted_iota(jnp.int32, mixed.shape, 0) % span < length
    mixed = jnp.where(live, mixed / total, 0.0).astype(jnp.bfloat16)
    for h in range(heads):
        out_ref[0, :, h * HEAD_SIZE : (h + 1) * HEAD_SIZE] = mixed[h * span : (h + 1) * span]


def attention(span, q_width, projected, cache, keep_flag, destination, row_counts):
    cosine, sine = rope_tables(span, PROMPT_TOKENS)
    cosine = jnp.concatenate([cosine, cosine], axis=1)
    sine = jnp.concatenate([-sine, sine], axis=1)
    heads = q_width // HEAD_SIZE
    smem = pl.BlockSpec(memory_space=pltpu.SMEM)
    table = pl.BlockSpec((span, HEAD_SIZE), lambda s, p: (0, 0))
    return pl.pallas_call(
        attention_kernel,
        grid=(OUT_DEV, heads // 2),
        out_shape=jax.ShapeDtypeStruct((OUT_DEV, span, q_width), jnp.bfloat16),
        in_specs=[
            smem,
            smem,
            smem,
            table,
            table,
            pl.BlockSpec((span, 2 * HEAD_SIZE), lambda s, p: (s, p)),
            pl.BlockSpec((span, HEAD_SIZE), lambda s, p: (s, heads)),
            pl.BlockSpec((span, HEAD_SIZE), lambda s, p: (s, heads + 1)),
            pl.BlockSpec(cache.shape, lambda s, p: (0, 0, 0, 0)),
        ],
        out_specs=pl.BlockSpec((1, span, 2 * HEAD_SIZE), lambda s, p: (s, 0, p)),
        compiler_params=pltpu.CompilerParams(vmem_limit_bytes=48 * 1024 * 1024),
        name="attend",
    )(
        keep_flag,
        destination,
        row_counts,
        cosine,
        sine,
        projected,
        projected,
        projected,
        cache,
    )


def body(
    groups,
    shards,
    hidden,
    norm_gain,
    w_query,
    key_projection_weight,
    value_projection_weight,
    prompt_key_cache,
    prompt_value_cache,
    keep_flag,
    destination,
    row_counts,
):
    projected, cache = project(
        shards,
        groups,
        hidden,
        norm_gain,
        w_query,
        key_projection_weight,
        value_projection_weight,
        prompt_key_cache,
        prompt_value_cache,
        keep_flag,
        destination,
    )
    return attention(
        hidden.shape[1], w_query.shape[1], projected, cache, keep_flag, destination, row_counts
    )


def solution(mesh):
    return jax.shard_map(
        functools.partial(body, mesh.shape["group"], mesh.shape["fsdp"]),
        mesh=mesh,
        in_specs=(
            P("group", None, "fsdp"),
            P(),
            P("group", "fsdp"),
            P("group", None),
            P("group", None),
            P("group", None),
            P("group", None),
            P(),
            P(),
            P(),
        ),
        out_specs=P("group", None, "fsdp"),
        check_vma=False,
    )
```

```python
import functools
import math

import jax
import jax.numpy as jnp
from jax import lax
from jax.experimental import pallas as pl
from jax.experimental.pallas import tpu as pltpu
from jax.sharding import PartitionSpec as P

QUERY_HEADS = 64
KEY_VALUE_HEADS = 8
HEAD_SIZE = 128
PROMPT_TOKENS = 2048
IN_DEV = 8
CAP = 1
OUT_DEV = 4


EPSILON = 1e-05
ROPE_THETA = 500000.0
CONTEXT_BASE = 8192.0
STRETCH = 8.0
MASKED_SCORE = -1e30


def rope_tables(length, offset):
    half_dim = HEAD_SIZE // 2
    base_rate = ROPE_THETA ** (-(jnp.arange(half_dim, dtype=jnp.float32) * 2.0 / HEAD_SIZE))
    ratio = CONTEXT_BASE * base_rate / (2.0 * jnp.pi)
    smooth = jnp.clip((ratio - 1.0) / 3.0, 0.0, 1.0)
    inverse_rate = (1.0 - smooth) * base_rate / STRETCH + smooth * base_rate
    token_positions = jnp.arange(length, dtype=jnp.float32) + offset
    angles = token_positions[:, None] * inverse_rate[None, :]
    return (jnp.cos(angles), jnp.sin(angles))


ROW_TILE = 16
PAIR = 2 * HEAD_SIZE
GEMM_ROWS = 256
MESH = pl.DeviceIdType.MESH


def sublayer_kernel(
    shape,
    keep_ref,
    dest_ref,
    counts_ref,
    hidden_ref,
    gain_ref,
    cos_ref,
    sin_ref,
    wq_ref,
    wk_ref,
    wv_ref,
    kc_ref,
    vc_ref,
    out_ref,
    outbox,
    inbox,
    x_all,
    x_norm,
    cache,
    q_rows,
    new_keys,
    new_values,
    local_sem,
    inbox_send,
    inbox_recv,
    x_send,
    x_recv,
    w_send,
    w_recv,
    *w_all,
):
    groups, shards, lines, width = shape
    columns = shards // lines
    chips = groups // 2
    features = hidden_ref.shape[2]
    span = hidden_ref.shape[1]
    depth = wq_ref.shape[0]
    pairs = wq_ref.shape[1] // PAIR
    cached_chunk = pairs + 1
    heads = wq_ref.shape[1] // HEAD_SIZE
    group = lax.axis_index("group")
    shard = lax.axis_index("fsdp")
    chip, core = group // 2, group % 2
    col, line = shard // lines, shard % lines
    head = shard * heads // (QUERY_HEADS // KEY_VALUE_HEADS)
    head_cols = pl.ds(pl.multiple_of(head * HEAD_SIZE, HEAD_SIZE), HEAD_SIZE)

    local = [
        [
            pltpu.make_async_copy(
                ref.at[:, head_cols], w_all[0].at[group, n], local_sem.at[0, n]
            )
            for n, ref in enumerate((wk_ref, wv_ref))
        ]
    ]
    for c in range(pairs):
        local.append(
            [
                pltpu.make_async_copy(
                    wq_ref.at[:, pl.ds((2 * c + n) * HEAD_SIZE, HEAD_SIZE)],
                    w_all[c + 1].at[group, n],
                    local_sem.at[c + 1, n],
                )
                for n in range(2)
            ]
        )
    local.append(
        [
            pltpu.make_async_copy(
                ref.at[:, head_cols], cache.at[group, n], local_sem.at[cached_chunk, n]
            )
            for n, ref in enumerate((kc_ref, vc_ref))
        ]
    )
    for copies in local:
        for copy in copies:
            copy.start()

    x_hops = [
        (col < columns - 1, shard + lines),
        (col > 0, shard - lines),
        (line < lines - 1, shard + 1),
        (line > 0, shard - 1),
    ]
    w_hops = [(chip < chips - 1, group + 2), (chip > 0, group - 2)]
    partner = chip * 2 + 1 - core

    barrier = pltpu.get_barrier_semaphore()
    for j in range(1, groups):
        pl.semaphore_signal(
            barrier, inc=1, device_id={"group": (group + j) % groups}, device_id_type=MESH
        )
    for valid, near in x_hops:

        @pl.when(valid)
        def _(near=near):
            pl.semaphore_signal(barrier, inc=1, device_id={"fsdp": near}, device_id_type=MESH)

    near_count = sum(jnp.where(valid, 1, 0) for valid, _ in x_hops)
    pl.semaphore_wait(barrier, groups - 1 + near_count)

    first = group * IN_DEV

    def chosen(target):
        index = jnp.int32(0)
        for b in range(IN_DEV):
            hit = (keep_ref[first + b] == 1) & (lax.div(dest_ref[first + b], OUT_DEV) == target)
            index = jnp.where(hit, b, index)
        return index

    posts = []
    for j in range(groups - 1, 0, -1):
        peer = (group + j) % groups
        outbox[j - 1] = hidden_ref[chosen(peer)]
        post = pltpu.make_async_remote_copy(
            src_ref=outbox.at[j - 1],
            dst_ref=inbox.at[group],
            send_sem=inbox_send.at[j - 1],
            recv_sem=inbox_recv.at[group],
            device_id={"group": peer},
            device_id_type=MESH,
        )
        post.start()
        posts.append(post)
    inbox[group] = hidden_ref[chosen(group)]

    sends = []

    def x_copy(unit, hop):
        return pltpu.make_async_remote_copy(
            src_ref=x_all.at[unit],
            dst_ref=x_all.at[unit],
            send_sem=x_send.at[unit, hop],
            recv_sem=x_recv.at[unit],
            device_id={"fsdp": x_hops[hop][1]},
            device_id_type=MESH,
        )

    def x_arrival(unit):
        return pltpu.make_async_remote_copy(
            src_ref=x_all.at[unit],
            dst_ref=x_all.at[unit],
            send_sem=x_send.at[unit, 0],
            recv_sem=x_recv.at[unit],
            device_id={"fsdp": (shard + 1) % shards},
            device_id_type=MESH,
        )

    def w_copy(unit, c, hop):
        ref = (cache if c == cached_chunk else w_all[c]).at[unit]
        return pltpu.make_async_remote_copy(
            src_ref=ref,
            dst_ref=ref,
            send_sem=w_send.at[unit, c, hop],
            recv_sem=w_recv.at[unit, c],
            device_id={"group": partner if hop == 2 else w_hops[hop][1]},
            device_id_type=MESH,
        )

    def launch(copy, when):
        @pl.when(when)
        def _():
            copy.start()

        sends.append((copy, when))

    always = group >= 0
    order = [cached_chunk] + list(range(pairs + 1))
    for c in order:
        for copy in local[c]:
            copy.wait()
        for hop in (0, 1):
            launch(w_copy(group, c, hop), w_hops[hop][0])
        launch(w_copy(group, c, 2), always)

    for j in range(1, groups):
        source = (group + j) % groups
        pltpu.make_async_remote_copy(
            src_ref=inbox.at[source],
            dst_ref=inbox.at[source],
            send_sem=inbox_send.at[j - 1],
            recv_sem=inbox_recv.at[source],
            device_id={"group": source},
            device_id_type=MESH,
        ).wait_recv()
    for o in range(OUT_DEV):
        slot = group * OUT_DEV + o

        def find(b, owner):
            hit = (keep_ref[b] == 1) & (dest_ref[b] == slot)
            return jnp.where(hit, lax.div(b, jnp.int32(IN_DEV)), owner)

        owner = lax.fori_loop(0, groups * IN_DEV, find, jnp.int32(0))
        x_all[shard, pl.ds(o * span, span), :] = inbox[owner]

    for hop in range(4):
        launch(x_copy(shard, hop), x_hops[hop][0])

    def x_column(step):
        for hop, sign in ((0, 1), (1, -1)):
            source = col - sign * step
            there = (source >= 0) & (source < columns)
            unit = source * lines + line

            @pl.when(there)
            def _(unit=unit):
                x_arrival(unit).wait_recv()

            if step < columns - 1:
                launch(x_copy(unit, hop), there & x_hops[hop][0])
            for side in (2, 3):
                launch(x_copy(unit, side), there & x_hops[side][0])

    def x_line(step):
        for hop, sign in ((2, 1), (3, -1)):
            source = line - sign * step
            there = (source >= 0) & (source < lines)
            for k in range(columns):
                unit = k * lines + source

                @pl.when(there)
                def _(unit=unit):
                    x_arrival(unit).wait_recv()

                if step < lines - 1:
                    launch(x_copy(unit, hop), there & x_hops[hop][0])

    def w_chip(step, c):
        for hop, sign in ((0, 1), (1, -1)):
            source = chip - sign * step
            there = (source >= 0) & (source < chips)
            unit = source * 2 + core

            @pl.when(there)
            def _(unit=unit):
                w_copy(unit, c, 2).wait_recv()

            if step < chips - 1:
                launch(w_copy(unit, c, hop), there & w_hops[hop][0])
            launch(w_copy(unit, c, 2), there)

    w_events = [(step, c) for c in order for step in range(1, chips)]
    w_chip(*w_events.pop(0))
    for step in range(1, columns):
        x_column(step)
        if len(w_events) > 2:
            w_chip(*w_events.pop(0))
    for step in range(1, lines):
        x_line(step)

    def normalize(i, carry):
        rows = pl.ds(pl.multiple_of(i * ROW_TILE, ROW_TILE), ROW_TILE)
        total = jnp.zeros((ROW_TILE, features), jnp.float32)
        for f in range(shards):
            values = x_all[f, rows, :].astype(jnp.float32)
            total = total + values * values
        mean = jnp.sum(total, axis=1, keepdims=True) / width
        factor = lax.rsqrt(mean + EPSILON)
        for f in range(shards):
            values = x_all[f, rows, :].astype(jnp.float32)
            x_norm[f, rows, :] = (values * factor * gain_ref[pl.ds(f, 1), :]).astype(jnp.bfloat16)
        return carry

    lax.fori_loop(0, OUT_DEV * span // ROW_TILE, normalize, 0)

    def arrive(position):
        last = order[min(position, len(order) - 1)]
        while any(c == last for _, c in w_events):
            w_chip(*w_events.pop(0))

    def from_partner(c):
        for d in range(chips):
            w_copy((chip + d) % chips * 2 + 1 - core, c, 2).wait_recv()

    def multiply(c):
        def tile(m, carry):
            rows = pl.ds(pl.multiple_of(m * GEMM_ROWS, GEMM_ROWS), GEMM_ROWS)
            total = jnp.zeros((GEMM_ROWS, PAIR), jnp.float32)
            for f in range(shards):
                unit = f * features // depth
                inner = pl.ds(f * features % depth, features)
                both = jnp.concatenate(
                    [w_all[c][unit, 0, inner, :], w_all[c][unit, 1, inner, :]], axis=1
                )
                total = total + jnp.dot(
                    x_norm[f, rows, :], both, preferred_element_type=jnp.float32
                )
            q_rows[rows, :] = total
            return carry

        lax.fori_loop(0, OUT_DEV * span // GEMM_ROWS, tile, 0)

    def turn(values):
        return (
            values * cos_ref[...] + pltpu.roll(values, HEAD_SIZE // 2, 1) * sin_ref[...]
        ).astype(jnp.bfloat16)

    def keep_fresh(s, carry):
        rows = pl.ds(pl.multiple_of(s * span, span), span)
        new_keys[rows, :] = turn(q_rows[rows, pl.ds(0, HEAD_SIZE)])
        new_values[rows, :] = q_rows[rows, pl.ds(HEAD_SIZE, HEAD_SIZE)].astype(jnp.bfloat16)
        return carry

    contract = (((1,), (1,)), ((), ()))
    rate = HEAD_SIZE ** (-0.5) * math.log2(math.e)

    def attend(pair):
        def one_slot(s, carry):
            slot = group * OUT_DEV + s

            def find(b, length):
                hit = (keep_ref[b] == 1) & (dest_ref[b] == slot)
                return jnp.where(hit, counts_ref[b], length)

            length = lax.fori_loop(0, groups * IN_DEV, find, jnp.int32(0))
            rows = pl.ds(pl.multiple_of(s * span, span), span)
            queries = jnp.concatenate(
                [turn(q_rows[rows, pl.ds(h * HEAD_SIZE, HEAD_SIZE)]) for h in range(2)], axis=0
            )
            tokens = groups * cache.shape[2]
            prompt_keys = cache[:, 0].reshape(tokens, HEAD_SIZE)
            prompt_values = cache[:, 1].reshape(tokens, HEAD_SIZE)
            cached = lax.dot_general(
                queries, prompt_keys, contract, preferred_element_type=jnp.float32
            )
            fresh = lax.dot_general(
                queries, new_keys[rows, :], contract, preferred_element_type=jnp.float32
            )
            row = lax.broadcasted_iota(jnp.int32, fresh.shape, 0) % span
            column = lax.broadcasted_iota(jnp.int32, fresh.shape, 1)
            fresh = jnp.where((column <= row) & (column < length), fresh, MASKED_SCORE)
            top = jnp.maximum(
                jnp.max(cached, axis=1, keepdims=True), jnp.max(fresh, axis=1, keepdims=True)
            )
            cached = jnp.exp2((cached - top) * rate)
            fresh = jnp.exp2((fresh - top) * rate)
            total = jnp.sum(cached, axis=1, keepdims=True) + jnp.sum(fresh, axis=1, keepdims=True)
            mixed = jnp.dot(
                cached.astype(jnp.bfloat16), prompt_values, preferred_element_type=jnp.float32
            ) + jnp.dot(
                fresh.astype(jnp.bfloat16), new_values[rows, :], preferred_element_type=jnp.float32
            )
            live = lax.broadcasted_iota(jnp.int32, mixed.shape, 0) % span < length
            mixed = jnp.where(live, mixed / total, 0.0).astype(jnp.bfloat16)
            for h in range(2):
                columns_out = pl.ds(pair * PAIR + h * HEAD_SIZE, HEAD_SIZE)
                out_ref[s, :, columns_out] = mixed[h * span : (h + 1) * span]
            return carry

        lax.fori_loop(0, OUT_DEV, one_slot, 0)

    arrive(0)
    from_partner(cached_chunk)
    for c in range(pairs + 1):
        arrive(c + 2)
        from_partner(c)
        multiply(c)
        if c == 0:
            lax.fori_loop(0, OUT_DEV, keep_fresh, 0)
        else:
            attend(c - 1)
    for post in posts:
        post.wait_send()
    for copy, when in sends:

        @pl.when(when)
        def _(copy=copy):
            copy.wait_send()


def sublayer(
    shards, groups, hidden, norm_gain, w_query, wk, wv, kc, vc, keep_flag, destination, row_counts
):
    blocks, span, features = hidden.shape
    depth, q_width = w_query.shape
    width = norm_gain.shape[0]
    lines = math.isqrt(shards // 2)
    rows = OUT_DEV * span
    pairs = q_width // PAIR
    cached = kc.shape[0]
    cosine, sine = rope_tables(span, PROMPT_TOKENS)
    smem = pl.BlockSpec(memory_space=pltpu.SMEM)
    vmem = pl.BlockSpec(memory_space=pltpu.VMEM)
    anywhere = pl.BlockSpec(memory_space=pl.ANY)
    dma = pltpu.SemaphoreType.DMA
    return pl.pallas_call(
        functools.partial(sublayer_kernel, (groups, shards, lines, width)),
        out_shape=jax.ShapeDtypeStruct((OUT_DEV, span, q_width), jnp.bfloat16),
        in_specs=[smem] * 3 + [vmem] * 4 + [anywhere] * 5,
        out_specs=vmem,
        scratch_shapes=[
            pltpu.VMEM((groups - 1, span, features), jnp.bfloat16),
            pltpu.VMEM((groups, span, features), jnp.bfloat16),
            pltpu.VMEM((shards, rows, features), jnp.bfloat16),
            pltpu.VMEM((shards, rows, features), jnp.bfloat16),
            pltpu.VMEM((groups, 2, cached, HEAD_SIZE), jnp.bfloat16),
            pltpu.VMEM((rows, PAIR), jnp.float32),
            pltpu.VMEM((rows, HEAD_SIZE), jnp.bfloat16),
            pltpu.VMEM((rows, HEAD_SIZE), jnp.bfloat16),
            dma((pairs + 2, 2)),
            dma((groups - 1,)),
            dma((groups,)),
            dma((shards, 4)),
            dma((shards,)),
            dma((groups, pairs + 2, 3)),
            dma((groups, pairs + 2)),
        ]
        + [pltpu.VMEM((groups, 2, depth, HEAD_SIZE), jnp.bfloat16)] * (pairs + 1),
        compiler_params=pltpu.CompilerParams(
            collective_id=0, has_side_effects=True, vmem_limit_bytes=60 * 1024 * 1024
        ),
        cost_estimate=pl.CostEstimate(
            flops=2 * rows * width * (q_width + PAIR),
            bytes_accessed=depth * (q_width + PAIR) * 2,
            transcendentals=0,
        ),
        name="gather_project_attend",
    )(
        keep_flag,
        destination,
        row_counts,
        hidden,
        norm_gain.astype(jnp.float32).reshape(shards, features),
        jnp.concatenate([cosine, cosine], axis=1),
        jnp.concatenate([-sine, sine], axis=1),
        w_query,
        wk,
        wv,
        kc,
        vc,
    )


def body(
    groups,
    shards,
    hidden,
    norm_gain,
    w_query,
    key_projection_weight,
    value_projection_weight,
    prompt_key_cache,
    prompt_value_cache,
    keep_flag,
    destination,
    row_counts,
):
    return sublayer(
        shards,
        groups,
        hidden,
        norm_gain,
        w_query,
        key_projection_weight,
        value_projection_weight,
        prompt_key_cache,
        prompt_value_cache,
        keep_flag,
        destination,
        row_counts,
    )


def solution(mesh):
    return jax.shard_map(
        functools.partial(body, mesh.shape["group"], mesh.shape["fsdp"]),
        mesh=mesh,
        in_specs=(
            P("group", None, "fsdp"),
            P(),
            P("group", "fsdp"),
            P("group", None),
            P("group", None),
            P("group", None),
            P("group", None),
            P(),
            P(),
            P(),
        ),
        out_specs=P("group", None, "fsdp"),
        check_vma=False,
    )
```

```python
import functools
import math

import jax
import jax.numpy as jnp
from jax import lax
from jax.experimental import pallas as pl
from jax.experimental.pallas import tpu as pltpu
from jax.sharding import PartitionSpec as P

QUERY_HEADS = 64
KEY_VALUE_HEADS = 8
HEAD_SIZE = 128
PROMPT_TOKENS = 2048
IN_DEV = 8
CAP = 1
OUT_DEV = 4


EPSILON = 1e-05
ROPE_THETA = 500000.0
CONTEXT_BASE = 8192.0
STRETCH = 8.0
MASKED_SCORE = -1e30


def rope_tables(length, offset):
    half_dim = HEAD_SIZE // 2
    base_rate = ROPE_THETA ** (-(jnp.arange(half_dim, dtype=jnp.float32) * 2.0 / HEAD_SIZE))
    ratio = CONTEXT_BASE * base_rate / (2.0 * jnp.pi)
    smooth = jnp.clip((ratio - 1.0) / 3.0, 0.0, 1.0)
    inverse_rate = (1.0 - smooth) * base_rate / STRETCH + smooth * base_rate
    token_positions = jnp.arange(length, dtype=jnp.float32) + offset
    angles = token_positions[:, None] * inverse_rate[None, :]
    return (jnp.cos(angles), jnp.sin(angles))


ROW_TILE = 16
PAIR = 2 * HEAD_SIZE
HALF_SLOTS = OUT_DEV // 2
MESH = pl.DeviceIdType.MESH


def sublayer_kernel(
    shape,
    keep_ref,
    dest_ref,
    counts_ref,
    hidden_ref,
    gain_ref,
    cos_ref,
    sin_ref,
    wq_ref,
    wk_ref,
    wv_ref,
    kc_ref,
    vc_ref,
    out_ref,
    outbox,
    inbox,
    x_first,
    x_second,
    x_norm,
    cache,
    q_rows,
    new_keys,
    new_values,
    local_sem,
    inbox_send,
    inbox_recv,
    x_send,
    x_recv,
    w_send,
    w_recv,
    *w_all,
):
    groups, shards, lines, width = shape
    columns = shards // lines
    chips = groups // 2
    features = hidden_ref.shape[2]
    span = hidden_ref.shape[1]
    depth = wq_ref.shape[0]
    half_rows = HALF_SLOTS * span
    x_all = (x_first, x_second)
    pairs = wq_ref.shape[1] // PAIR
    cached_chunk = pairs + 1
    heads = wq_ref.shape[1] // HEAD_SIZE
    group = lax.axis_index("group")
    shard = lax.axis_index("fsdp")
    chip, core = group // 2, group % 2
    col, line = shard // lines, shard % lines
    head = shard * heads // (QUERY_HEADS // KEY_VALUE_HEADS)
    head_cols = pl.ds(pl.multiple_of(head * HEAD_SIZE, HEAD_SIZE), HEAD_SIZE)

    local = [
        [
            pltpu.make_async_copy(
                ref.at[:, head_cols], w_all[0].at[group, n], local_sem.at[0, n]
            )
            for n, ref in enumerate((wk_ref, wv_ref))
        ]
    ]
    for c in range(pairs):
        local.append(
            [
                pltpu.make_async_copy(
                    wq_ref.at[:, pl.ds((2 * c + n) * HEAD_SIZE, HEAD_SIZE)],
                    w_all[c + 1].at[group, n],
                    local_sem.at[c + 1, n],
                )
                for n in range(2)
            ]
        )
    local.append(
        [
            pltpu.make_async_copy(
                ref.at[:, head_cols], cache.at[group, n], local_sem.at[cached_chunk, n]
            )
            for n, ref in enumerate((kc_ref, vc_ref))
        ]
    )
    for copies in local:
        for copy in copies:
            copy.start()

    x_hops = [
        (col < columns - 1, shard + lines),
        (col > 0, shard - lines),
        (line < lines - 1, shard + 1),
        (line > 0, shard - 1),
    ]
    w_hops = [(chip < chips - 1, group + 2), (chip > 0, group - 2)]
    partner = chip * 2 + 1 - core

    barrier = pltpu.get_barrier_semaphore()
    for j in range(1, groups):
        pl.semaphore_signal(
            barrier, inc=1, device_id={"group": (group + j) % groups}, device_id_type=MESH
        )
    for valid, near in x_hops:

        @pl.when(valid)
        def _(near=near):
            pl.semaphore_signal(barrier, inc=1, device_id={"fsdp": near}, device_id_type=MESH)

    near_count = sum(jnp.where(valid, 1, 0) for valid, _ in x_hops)
    pl.semaphore_wait(barrier, groups - 1 + near_count)

    first = group * IN_DEV

    def chosen(target):
        index = jnp.int32(0)
        for b in range(IN_DEV):
            hit = (keep_ref[first + b] == 1) & (lax.div(dest_ref[first + b], OUT_DEV) == target)
            index = jnp.where(hit, b, index)
        return index

    posts = []
    for j in range(groups - 1, 0, -1):
        peer = (group + j) % groups
        outbox[j - 1] = hidden_ref[chosen(peer)]
        post = pltpu.make_async_remote_copy(
            src_ref=outbox.at[j - 1],
            dst_ref=inbox.at[group],
            send_sem=inbox_send.at[j - 1],
            recv_sem=inbox_recv.at[group],
            device_id={"group": peer},
            device_id_type=MESH,
        )
        post.start()
        posts.append(post)
    inbox[group] = hidden_ref[chosen(group)]

    sends = []

    def x_copy(half, unit, hop):
        return pltpu.make_async_remote_copy(
            src_ref=x_all[half].at[unit],
            dst_ref=x_all[half].at[unit],
            send_sem=x_send.at[half, unit, hop],
            recv_sem=x_recv.at[half, unit],
            device_id={"fsdp": x_hops[hop][1]},
            device_id_type=MESH,
        )

    def x_arrival(half, unit):
        return pltpu.make_async_remote_copy(
            src_ref=x_all[half].at[unit],
            dst_ref=x_all[half].at[unit],
            send_sem=x_send.at[half, unit, 0],
            recv_sem=x_recv.at[half, unit],
            device_id={"fsdp": (shard + 1) % shards},
            device_id_type=MESH,
        )

    def w_copy(unit, c, hop):
        ref = (cache if c == cached_chunk else w_all[c]).at[unit]
        return pltpu.make_async_remote_copy(
            src_ref=ref,
            dst_ref=ref,
            send_sem=w_send.at[unit, c, hop],
            recv_sem=w_recv.at[unit, c],
            device_id={"group": partner if hop == 2 else w_hops[hop][1]},
            device_id_type=MESH,
        )

    def launch(copy, when):
        @pl.when(when)
        def _():
            copy.start()

        sends.append((copy, when))

    always = group >= 0
    order = [cached_chunk] + list(range(pairs + 1))
    for c in order:
        for copy in local[c]:
            copy.wait()
        for hop in (0, 1):
            launch(w_copy(group, c, hop), w_hops[hop][0])
        launch(w_copy(group, c, 2), always)

    for j in range(1, groups):
        source = (group + j) % groups
        pltpu.make_async_remote_copy(
            src_ref=inbox.at[source],
            dst_ref=inbox.at[source],
            send_sem=inbox_send.at[j - 1],
            recv_sem=inbox_recv.at[source],
            device_id={"group": source},
            device_id_type=MESH,
        ).wait_recv()
    for o in range(OUT_DEV):
        slot = group * OUT_DEV + o

        def find(b, owner):
            hit = (keep_ref[b] == 1) & (dest_ref[b] == slot)
            return jnp.where(hit, lax.div(b, jnp.int32(IN_DEV)), owner)

        owner = lax.fori_loop(0, groups * IN_DEV, find, jnp.int32(0))
        x_all[o // HALF_SLOTS][shard, pl.ds(o % HALF_SLOTS * span, span), :] = inbox[owner]

    def x_own(half):
        for hop in range(4):
            launch(x_copy(half, shard, hop), x_hops[hop][0])

    def x_column(step, half):
        for hop, sign in ((0, 1), (1, -1)):
            source = col - sign * step
            there = (source >= 0) & (source < columns)
            unit = source * lines + line

            @pl.when(there)
            def _(unit=unit):
                x_arrival(half, unit).wait_recv()

            if step < columns - 1:
                launch(x_copy(half, unit, hop), there & x_hops[hop][0])
            for side in (2, 3):
                launch(x_copy(half, unit, side), there & x_hops[side][0])

    def x_line(step, half):
        for hop, sign in ((2, 1), (3, -1)):
            source = line - sign * step
            there = (source >= 0) & (source < lines)
            for k in range(columns):
                unit = k * lines + source

                @pl.when(there)
                def _(unit=unit):
                    x_arrival(half, unit).wait_recv()

                if step < lines - 1:
                    launch(x_copy(half, unit, hop), there & x_hops[hop][0])

    def w_chip(step, c):
        for hop, sign in ((0, 1), (1, -1)):
            source = chip - sign * step
            there = (source >= 0) & (source < chips)
            unit = source * 2 + core

            @pl.when(there)
            def _(unit=unit):
                w_copy(unit, c, 2).wait_recv()

            if step < chips - 1:
                launch(w_copy(unit, c, hop), there & w_hops[hop][0])
            launch(w_copy(unit, c, 2), there)

    w_events = [(step, c) for c in order for step in range(1, chips)]
    def normalize(half):
        def tile(i, carry):
            start = pl.multiple_of(i * ROW_TILE, ROW_TILE)
            rows = pl.ds(start, ROW_TILE)
            rows_out = pl.ds(half * half_rows + start, ROW_TILE)
            total = jnp.zeros((ROW_TILE, features), jnp.float32)
            for f in range(shards):
                values = x_all[half][f, rows, :].astype(jnp.float32)
                total = total + values * values
            mean = jnp.sum(total, axis=1, keepdims=True) / width
            factor = lax.rsqrt(mean + EPSILON)
            for f in range(shards):
                values = x_all[half][f, rows, :].astype(jnp.float32)
                x_norm[f, rows_out, :] = (values * factor * gain_ref[pl.ds(f, 1), :]).astype(
                    jnp.bfloat16
                )
            return carry

        lax.fori_loop(0, half_rows // ROW_TILE, tile, 0)

    def arrive(last):
        while any(c == last for _, c in w_events):
            w_chip(*w_events.pop(0))

    def from_partner(c):
        for d in range(chips):
            w_copy((chip + d) % chips * 2 + 1 - core, c, 2).wait_recv()

    def multiply(c, half):
        rows = pl.ds(half * half_rows, half_rows)
        total = jnp.zeros((half_rows, PAIR), jnp.float32)
        for f in range(shards):
            unit = f * features // depth
            inner = pl.ds(f * features % depth, features)
            both = jnp.concatenate(
                [w_all[c][unit, 0, inner, :], w_all[c][unit, 1, inner, :]], axis=1
            )
            total = total + jnp.dot(x_norm[f, rows, :], both, preferred_element_type=jnp.float32)
        q_rows[rows, :] = total

    def turn(values):
        return (
            values * cos_ref[...] + pltpu.roll(values, HEAD_SIZE // 2, 1) * sin_ref[...]
        ).astype(jnp.bfloat16)

    def keep_fresh(s, carry):
        rows = pl.ds(pl.multiple_of(s * span, span), span)
        new_keys[rows, :] = turn(q_rows[rows, pl.ds(0, HEAD_SIZE)])
        new_values[rows, :] = q_rows[rows, pl.ds(HEAD_SIZE, HEAD_SIZE)].astype(jnp.bfloat16)
        return carry

    contract = (((1,), (1,)), ((), ()))
    rate = HEAD_SIZE ** (-0.5) * math.log2(math.e)

    def attend(pair, half):
        def one_slot(s, carry):
            slot = group * OUT_DEV + s

            def find(b, length):
                hit = (keep_ref[b] == 1) & (dest_ref[b] == slot)
                return jnp.where(hit, counts_ref[b], length)

            length = lax.fori_loop(0, groups * IN_DEV, find, jnp.int32(0))
            rows = pl.ds(pl.multiple_of(s * span, span), span)
            queries = jnp.concatenate(
                [turn(q_rows[rows, pl.ds(h * HEAD_SIZE, HEAD_SIZE)]) for h in range(2)], axis=0
            )
            tokens = groups * cache.shape[2]
            prompt_keys = cache[:, 0].reshape(tokens, HEAD_SIZE)
            prompt_values = cache[:, 1].reshape(tokens, HEAD_SIZE)
            cached = lax.dot_general(
                queries, prompt_keys, contract, preferred_element_type=jnp.float32
            )
            fresh = lax.dot_general(
                queries, new_keys[rows, :], contract, preferred_element_type=jnp.float32
            )
            row = lax.broadcasted_iota(jnp.int32, fresh.shape, 0) % span
            column = lax.broadcasted_iota(jnp.int32, fresh.shape, 1)
            fresh = jnp.where((column <= row) & (column < length), fresh, MASKED_SCORE)
            top = jnp.maximum(
                jnp.max(cached, axis=1, keepdims=True), jnp.max(fresh, axis=1, keepdims=True)
            )
            cached = jnp.exp2((cached - top) * rate)
            fresh = jnp.exp2((fresh - top) * rate)
            total = jnp.sum(cached, axis=1, keepdims=True) + jnp.sum(fresh, axis=1, keepdims=True)
            mixed = jnp.dot(
                cached.astype(jnp.bfloat16), prompt_values, preferred_element_type=jnp.float32
            ) + jnp.dot(
                fresh.astype(jnp.bfloat16), new_values[rows, :], preferred_element_type=jnp.float32
            )
            live = lax.broadcasted_iota(jnp.int32, mixed.shape, 0) % span < length
            mixed = jnp.where(live, mixed / total, 0.0).astype(jnp.bfloat16)
            for h in range(2):
                columns_out = pl.ds(pair * PAIR + h * HEAD_SIZE, HEAD_SIZE)
                out_ref[s, :, columns_out] = mixed[h * span : (h + 1) * span]
            return carry

        lax.fori_loop(half * HALF_SLOTS, (half + 1) * HALF_SLOTS, one_slot, 0)

    def keys_and_values(half):
        multiply(0, half)
        lax.fori_loop(half * HALF_SLOTS, (half + 1) * HALF_SLOTS, keep_fresh, 0)

    def heads_of(c, half):
        multiply(c, half)
        attend(c - 1, half)

    x_own(0)
    arrive(cached_chunk)
    for step in range(1, columns):
        x_column(step, 0)
        if step == columns - 2:
            arrive(0)
    arrive(0)
    x_own(1)
    x_column(1, 1)
    for step in range(1, lines):
        x_line(step, 0)
    normalize(0)
    from_partner(cached_chunk)
    from_partner(0)
    keys_and_values(0)
    ahead = 0
    for step in range(2, columns):
        x_column(step, 1)
        if ahead < pairs - 2:
            ahead += 1
            arrive(ahead)
            from_partner(ahead)
            heads_of(ahead, 0)
    for step in range(1, lines):
        x_line(step, 1)
    normalize(1)
    keys_and_values(1)
    arrive(ahead + 1)
    for c in range(1, ahead + 1):
        heads_of(c, 1)
    for c in range(ahead + 1, pairs + 1):
        from_partner(c)
        heads_of(c, 0)
        if c < pairs:
            arrive(c + 1)
        heads_of(c, 1)
    for post in posts:
        post.wait_send()
    for copy, when in sends:

        @pl.when(when)
        def _(copy=copy):
            copy.wait_send()


def sublayer(
    shards, groups, hidden, norm_gain, w_query, wk, wv, kc, vc, keep_flag, destination, row_counts
):
    blocks, span, features = hidden.shape
    depth, q_width = w_query.shape
    width = norm_gain.shape[0]
    lines = math.isqrt(shards // 2)
    rows = OUT_DEV * span
    pairs = q_width // PAIR
    cached = kc.shape[0]
    cosine, sine = rope_tables(span, PROMPT_TOKENS)
    smem = pl.BlockSpec(memory_space=pltpu.SMEM)
    vmem = pl.BlockSpec(memory_space=pltpu.VMEM)
    anywhere = pl.BlockSpec(memory_space=pl.ANY)
    dma = pltpu.SemaphoreType.DMA
    return pl.pallas_call(
        functools.partial(sublayer_kernel, (groups, shards, lines, width)),
        out_shape=jax.ShapeDtypeStruct((OUT_DEV, span, q_width), jnp.bfloat16),
        in_specs=[smem] * 3 + [vmem] * 4 + [anywhere] * 5,
        out_specs=vmem,
        scratch_shapes=[
            pltpu.VMEM((groups - 1, span, features), jnp.bfloat16),
            pltpu.VMEM((groups, span, features), jnp.bfloat16),
            pltpu.VMEM((shards, rows // 2, features), jnp.bfloat16),
            pltpu.VMEM((shards, rows // 2, features), jnp.bfloat16),
            pltpu.VMEM((shards, rows, features), jnp.bfloat16),
            pltpu.VMEM((groups, 2, cached, HEAD_SIZE), jnp.bfloat16),
            pltpu.VMEM((rows, PAIR), jnp.float32),
            pltpu.VMEM((rows, HEAD_SIZE), jnp.bfloat16),
            pltpu.VMEM((rows, HEAD_SIZE), jnp.bfloat16),
            dma((pairs + 2, 2)),
            dma((groups - 1,)),
            dma((groups,)),
            dma((2, shards, 4)),
            dma((2, shards)),
            dma((groups, pairs + 2, 3)),
            dma((groups, pairs + 2)),
        ]
        + [pltpu.VMEM((groups, 2, depth, HEAD_SIZE), jnp.bfloat16)] * (pairs + 1),
        compiler_params=pltpu.CompilerParams(
            collective_id=0, has_side_effects=True, vmem_limit_bytes=60 * 1024 * 1024
        ),
        cost_estimate=pl.CostEstimate(
            flops=2 * rows * width * (q_width + PAIR),
            bytes_accessed=depth * (q_width + PAIR) * 2,
            transcendentals=0,
        ),
        name="gather_project_attend",
    )(
        keep_flag,
        destination,
        row_counts,
        hidden,
        norm_gain.astype(jnp.float32).reshape(shards, features),
        jnp.concatenate([cosine, cosine], axis=1),
        jnp.concatenate([-sine, sine], axis=1),
        w_query,
        wk,
        wv,
        kc,
        vc,
    )


def body(
    groups,
    shards,
    hidden,
    norm_gain,
    w_query,
    key_projection_weight,
    value_projection_weight,
    prompt_key_cache,
    prompt_value_cache,
    keep_flag,
    destination,
    row_counts,
):
    return sublayer(
        shards,
        groups,
        hidden,
        norm_gain,
        w_query,
        key_projection_weight,
        value_projection_weight,
        prompt_key_cache,
        prompt_value_cache,
        keep_flag,
        destination,
        row_counts,
    )


def solution(mesh):
    return jax.shard_map(
        functools.partial(body, mesh.shape["group"], mesh.shape["fsdp"]),
        mesh=mesh,
        in_specs=(
            P("group", None, "fsdp"),
            P(),
            P("group", "fsdp"),
            P("group", None),
            P("group", None),
            P("group", None),
            P("group", None),
            P(),
            P(),
            P(),
        ),
        out_specs=P("group", None, "fsdp"),
        check_vma=False,
    )
```

```python
import functools
import math

import jax
import jax.numpy as jnp
from jax import lax
from jax.experimental import pallas as pl
from jax.experimental.pallas import tpu as pltpu
from jax.sharding import PartitionSpec as P

QUERY_HEADS = 64
KEY_VALUE_HEADS = 8
HEAD_SIZE = 128
PROMPT_TOKENS = 2048
IN_DEV = 8
CAP = 1
OUT_DEV = 4


EPSILON = 1e-05
ROPE_THETA = 500000.0
CONTEXT_BASE = 8192.0
STRETCH = 8.0
MASKED_SCORE = -1e30


def rope_tables(length, offset):
    half_dim = HEAD_SIZE // 2
    base_rate = ROPE_THETA ** (-(jnp.arange(half_dim, dtype=jnp.float32) * 2.0 / HEAD_SIZE))
    ratio = CONTEXT_BASE * base_rate / (2.0 * jnp.pi)
    smooth = jnp.clip((ratio - 1.0) / 3.0, 0.0, 1.0)
    inverse_rate = (1.0 - smooth) * base_rate / STRETCH + smooth * base_rate
    token_positions = jnp.arange(length, dtype=jnp.float32) + offset
    angles = token_positions[:, None] * inverse_rate[None, :]
    return (jnp.cos(angles), jnp.sin(angles))


ROW_TILE = 16
PAIR = 2 * HEAD_SIZE
HALF_SLOTS = OUT_DEV // 2
MESH = pl.DeviceIdType.MESH


def sublayer_kernel(
    shape,
    keep_ref,
    dest_ref,
    counts_ref,
    hidden_ref,
    gain_ref,
    cos_ref,
    sin_ref,
    wq_ref,
    wk_ref,
    wv_ref,
    kc_ref,
    vc_ref,
    out_ref,
    outbox,
    inbox,
    x_first,
    x_second,
    x_norm,
    cache,
    q_rows,
    new_keys,
    new_values,
    local_sem,
    inbox_send,
    inbox_recv,
    x_send,
    x_recv,
    w_send,
    w_recv,
    *w_all,
):
    groups, shards, lines, width = shape
    columns = shards // lines
    chips = groups // 2
    features = hidden_ref.shape[2]
    span = hidden_ref.shape[1]
    depth = wq_ref.shape[0]
    half_rows = HALF_SLOTS * span
    x_all = (x_first, x_second)
    pairs = wq_ref.shape[1] // PAIR
    cached_chunk = pairs + 1
    heads = wq_ref.shape[1] // HEAD_SIZE
    group = lax.axis_index("group")
    shard = lax.axis_index("fsdp")
    chip, core = group // 2, group % 2
    col, line = shard // lines, shard % lines
    head = shard * heads // (QUERY_HEADS // KEY_VALUE_HEADS)
    head_cols = pl.ds(pl.multiple_of(head * HEAD_SIZE, HEAD_SIZE), HEAD_SIZE)

    local = [
        [
            pltpu.make_async_copy(
                ref.at[:, head_cols], w_all[0].at[group, n], local_sem.at[0, n]
            )
            for n, ref in enumerate((wk_ref, wv_ref))
        ]
    ]
    for c in range(pairs):
        local.append(
            [
                pltpu.make_async_copy(
                    wq_ref.at[:, pl.ds((2 * c + n) * HEAD_SIZE, HEAD_SIZE)],
                    w_all[c + 1].at[group, n],
                    local_sem.at[c + 1, n],
                )
                for n in range(2)
            ]
        )
    local.append(
        [
            pltpu.make_async_copy(
                ref.at[:, head_cols], cache.at[group, n], local_sem.at[cached_chunk, n]
            )
            for n, ref in enumerate((kc_ref, vc_ref))
        ]
    )
    for copies in local:
        for copy in copies:
            copy.start()

    x_hops = [
        (col < columns - 1, shard + lines),
        (col > 0, shard - lines),
        (line < lines - 1, shard + 1),
        (line > 0, shard - 1),
    ]
    w_hops = [(chip < chips - 1, group + 2), (chip > 0, group - 2)]
    partner = chip * 2 + 1 - core

    barrier = pltpu.get_barrier_semaphore()
    for j in range(1, groups):
        pl.semaphore_signal(
            barrier, inc=1, device_id={"group": (group + j) % groups}, device_id_type=MESH
        )
    for valid, near in x_hops:

        @pl.when(valid)
        def _(near=near):
            pl.semaphore_signal(barrier, inc=1, device_id={"fsdp": near}, device_id_type=MESH)

    near_count = sum(jnp.where(valid, 1, 0) for valid, _ in x_hops)
    pl.semaphore_wait(barrier, groups - 1 + near_count)

    first = group * IN_DEV

    def chosen(target):
        index = jnp.int32(0)
        for b in range(IN_DEV):
            hit = (keep_ref[first + b] == 1) & (lax.div(dest_ref[first + b], OUT_DEV) == target)
            index = jnp.where(hit, b, index)
        return index

    posts = []
    for j in range(groups - 1, 0, -1):
        peer = (group + j) % groups
        outbox[j - 1] = hidden_ref[chosen(peer)]
        post = pltpu.make_async_remote_copy(
            src_ref=outbox.at[j - 1],
            dst_ref=inbox.at[group],
            send_sem=inbox_send.at[j - 1],
            recv_sem=inbox_recv.at[group],
            device_id={"group": peer},
            device_id_type=MESH,
        )
        post.start()
        posts.append(post)
    inbox[group] = hidden_ref[chosen(group)]

    sends = []

    def x_copy(half, unit, hop):
        return pltpu.make_async_remote_copy(
            src_ref=x_all[half].at[unit],
            dst_ref=x_all[half].at[unit],
            send_sem=x_send.at[half, unit, hop],
            recv_sem=x_recv.at[half, unit],
            device_id={"fsdp": x_hops[hop][1]},
            device_id_type=MESH,
        )

    def x_arrival(half, unit):
        return pltpu.make_async_remote_copy(
            src_ref=x_all[half].at[unit],
            dst_ref=x_all[half].at[unit],
            send_sem=x_send.at[half, unit, 0],
            recv_sem=x_recv.at[half, unit],
            device_id={"fsdp": (shard + 1) % shards},
            device_id_type=MESH,
        )

    def w_copy(unit, c, hop):
        ref = (cache if c == cached_chunk else w_all[c]).at[unit]
        return pltpu.make_async_remote_copy(
            src_ref=ref,
            dst_ref=ref,
            send_sem=w_send.at[unit, c, hop],
            recv_sem=w_recv.at[unit, c],
            device_id={"group": partner if hop == 2 else w_hops[hop][1]},
            device_id_type=MESH,
        )

    def launch(copy, when):
        @pl.when(when)
        def _():
            copy.start()

        sends.append((copy, when))

    always = group >= 0
    order = [cached_chunk] + list(range(pairs + 1))

    def w_own(position):
        if position < len(order):
            c = order[position]
            for copy in local[c]:
                copy.wait()
            for hop in (0, 1):
                launch(w_copy(group, c, hop), w_hops[hop][0])
            launch(w_copy(group, c, 2), always)

    w_own(0)
    w_own(1)

    for j in range(1, groups):
        source = (group + j) % groups
        pltpu.make_async_remote_copy(
            src_ref=inbox.at[source],
            dst_ref=inbox.at[source],
            send_sem=inbox_send.at[j - 1],
            recv_sem=inbox_recv.at[source],
            device_id={"group": source},
            device_id_type=MESH,
        ).wait_recv()
    for o in range(OUT_DEV):
        slot = group * OUT_DEV + o

        def find(b, owner):
            hit = (keep_ref[b] == 1) & (dest_ref[b] == slot)
            return jnp.where(hit, lax.div(b, jnp.int32(IN_DEV)), owner)

        owner = lax.fori_loop(0, groups * IN_DEV, find, jnp.int32(0))
        x_all[o // HALF_SLOTS][shard, pl.ds(o % HALF_SLOTS * span, span), :] = inbox[owner]

    def x_own(half):
        for hop in range(4):
            launch(x_copy(half, shard, hop), x_hops[hop][0])

    def x_column(step, half):
        for hop, sign in ((0, 1), (1, -1)):
            source = col - sign * step
            there = (source >= 0) & (source < columns)
            unit = source * lines + line

            @pl.when(there)
            def _(unit=unit):
                x_arrival(half, unit).wait_recv()

            if step < columns - 1:
                launch(x_copy(half, unit, hop), there & x_hops[hop][0])
            for side in (2, 3):
                launch(x_copy(half, unit, side), there & x_hops[side][0])

    def x_line(step, half):
        for hop, sign in ((2, 1), (3, -1)):
            source = line - sign * step
            there = (source >= 0) & (source < lines)
            for k in range(columns):
                unit = k * lines + source

                @pl.when(there)
                def _(unit=unit):
                    x_arrival(half, unit).wait_recv()

                if step < lines - 1:
                    launch(x_copy(half, unit, hop), there & x_hops[hop][0])

    def w_chip(step, c):
        for hop, sign in ((0, 1), (1, -1)):
            source = chip - sign * step
            there = (source >= 0) & (source < chips)
            unit = source * 2 + core

            @pl.when(there)
            def _(unit=unit):
                w_copy(unit, c, 2).wait_recv()

            if step < chips - 1:
                launch(w_copy(unit, c, hop), there & w_hops[hop][0])
            launch(w_copy(unit, c, 2), there)
        if step == 1:
            w_own(order.index(c) + 2)

    w_events = [(step, c) for c in order for step in range(1, chips)]
    def normalize(half):
        def tile(i, carry):
            start = pl.multiple_of(i * ROW_TILE, ROW_TILE)
            rows = pl.ds(start, ROW_TILE)
            rows_out = pl.ds(half * half_rows + start, ROW_TILE)
            total = jnp.zeros((ROW_TILE, features), jnp.float32)
            for f in range(shards):
                values = x_all[half][f, rows, :].astype(jnp.float32)
                total = total + values * values
            mean = jnp.sum(total, axis=1, keepdims=True) / width
            factor = lax.rsqrt(mean + EPSILON)
            for f in range(shards):
                values = x_all[half][f, rows, :].astype(jnp.float32)
                x_norm[f, rows_out, :] = (values * factor * gain_ref[pl.ds(f, 1), :]).astype(
                    jnp.bfloat16
                )
            return carry

        lax.fori_loop(0, half_rows // ROW_TILE, tile, 0)

    def arrive(last):
        while any(c == last for _, c in w_events):
            w_chip(*w_events.pop(0))

    def from_partner(c):
        for d in range(chips):
            w_copy((chip + d) % chips * 2 + 1 - core, c, 2).wait_recv()

    def multiply(c, half):
        rows = pl.ds(half * half_rows, half_rows)
        total = jnp.zeros((half_rows, PAIR), jnp.float32)
        for f in range(shards):
            unit = f * features // depth
            inner = pl.ds(f * features % depth, features)
            both = jnp.concatenate(
                [w_all[c][unit, 0, inner, :], w_all[c][unit, 1, inner, :]], axis=1
            )
            total = total + jnp.dot(x_norm[f, rows, :], both, preferred_element_type=jnp.float32)
        q_rows[rows, :] = total

    def turn(values):
        return (
            values * cos_ref[...] + pltpu.roll(values, HEAD_SIZE // 2, 1) * sin_ref[...]
        ).astype(jnp.bfloat16)

    def keep_fresh(s, carry):
        rows = pl.ds(pl.multiple_of(s * span, span), span)
        new_keys[rows, :] = turn(q_rows[rows, pl.ds(0, HEAD_SIZE)])
        new_values[rows, :] = q_rows[rows, pl.ds(HEAD_SIZE, HEAD_SIZE)].astype(jnp.bfloat16)
        return carry

    contract = (((1,), (1,)), ((), ()))
    rate = HEAD_SIZE ** (-0.5) * math.log2(math.e)

    def attend(pair, half):
        def one_slot(s, carry):
            slot = group * OUT_DEV + s

            def find(b, length):
                hit = (keep_ref[b] == 1) & (dest_ref[b] == slot)
                return jnp.where(hit, counts_ref[b], length)

            length = lax.fori_loop(0, groups * IN_DEV, find, jnp.int32(0))
            rows = pl.ds(pl.multiple_of(s * span, span), span)
            queries = jnp.concatenate(
                [turn(q_rows[rows, pl.ds(h * HEAD_SIZE, HEAD_SIZE)]) for h in range(2)], axis=0
            )
            tokens = groups * cache.shape[2]
            prompt_keys = cache[:, 0].reshape(tokens, HEAD_SIZE)
            prompt_values = cache[:, 1].reshape(tokens, HEAD_SIZE)
            cached = lax.dot_general(
                queries, prompt_keys, contract, preferred_element_type=jnp.float32
            )
            fresh = lax.dot_general(
                queries, new_keys[rows, :], contract, preferred_element_type=jnp.float32
            )
            row = lax.broadcasted_iota(jnp.int32, fresh.shape, 0) % span
            column = lax.broadcasted_iota(jnp.int32, fresh.shape, 1)
            fresh = jnp.where((column <= row) & (column < length), fresh, MASKED_SCORE)
            top = jnp.maximum(
                jnp.max(cached, axis=1, keepdims=True), jnp.max(fresh, axis=1, keepdims=True)
            )
            cached = jnp.exp2((cached - top) * rate)
            fresh = jnp.exp2((fresh - top) * rate)
            total = jnp.sum(cached, axis=1, keepdims=True) + jnp.sum(fresh, axis=1, keepdims=True)
            mixed = jnp.dot(
                cached.astype(jnp.bfloat16), prompt_values, preferred_element_type=jnp.float32
            ) + jnp.dot(
                fresh.astype(jnp.bfloat16), new_values[rows, :], preferred_element_type=jnp.float32
            )
            live = lax.broadcasted_iota(jnp.int32, mixed.shape, 0) % span < length
            mixed = jnp.where(live, mixed / total, 0.0).astype(jnp.bfloat16)
            for h in range(2):
                columns_out = pl.ds(pair * PAIR + h * HEAD_SIZE, HEAD_SIZE)
                out_ref[s, :, columns_out] = mixed[h * span : (h + 1) * span]
            return carry

        lax.fori_loop(half * HALF_SLOTS, (half + 1) * HALF_SLOTS, one_slot, 0)

    def keys_and_values(half):
        multiply(0, half)
        lax.fori_loop(half * HALF_SLOTS, (half + 1) * HALF_SLOTS, keep_fresh, 0)

    def heads_of(c, half):
        multiply(c, half)
        attend(c - 1, half)

    x_own(0)
    arrive(cached_chunk)
    for step in range(1, columns):
        x_column(step, 0)
        if step == columns - 2:
            arrive(0)
    arrive(0)
    x_own(1)
    x_column(1, 1)
    for step in range(1, lines):
        x_line(step, 0)
    normalize(0)
    from_partner(cached_chunk)
    from_partner(0)
    keys_and_values(0)
    ahead = 0
    for step in range(2, columns):
        x_column(step, 1)
        if ahead < pairs - 2:
            ahead += 1
            arrive(ahead)
            from_partner(ahead)
            heads_of(ahead, 0)
    for step in range(1, lines):
        x_line(step, 1)
    normalize(1)
    keys_and_values(1)
    arrive(ahead + 1)
    for c in range(1, ahead + 1):
        heads_of(c, 1)
    for c in range(ahead + 1, pairs + 1):
        from_partner(c)
        heads_of(c, 0)
        if c < pairs:
            arrive(c + 1)
        heads_of(c, 1)
    for post in posts:
        post.wait_send()
    for copy, when in sends:

        @pl.when(when)
        def _(copy=copy):
            copy.wait_send()


def sublayer(
    shards, groups, hidden, norm_gain, w_query, wk, wv, kc, vc, keep_flag, destination, row_counts
):
    blocks, span, features = hidden.shape
    depth, q_width = w_query.shape
    width = norm_gain.shape[0]
    lines = math.isqrt(shards // 2)
    rows = OUT_DEV * span
    pairs = q_width // PAIR
    cached = kc.shape[0]
    cosine, sine = rope_tables(span, PROMPT_TOKENS)
    smem = pl.BlockSpec(memory_space=pltpu.SMEM)
    vmem = pl.BlockSpec(memory_space=pltpu.VMEM)
    anywhere = pl.BlockSpec(memory_space=pl.ANY)
    dma = pltpu.SemaphoreType.DMA
    return pl.pallas_call(
        functools.partial(sublayer_kernel, (groups, shards, lines, width)),
        out_shape=jax.ShapeDtypeStruct((OUT_DEV, span, q_width), jnp.bfloat16),
        in_specs=[smem] * 3 + [vmem] * 4 + [anywhere] * 5,
        out_specs=vmem,
        scratch_shapes=[
            pltpu.VMEM((groups - 1, span, features), jnp.bfloat16),
            pltpu.VMEM((groups, span, features), jnp.bfloat16),
            pltpu.VMEM((shards, rows // 2, features), jnp.bfloat16),
            pltpu.VMEM((shards, rows // 2, features), jnp.bfloat16),
            pltpu.VMEM((shards, rows, features), jnp.bfloat16),
            pltpu.VMEM((groups, 2, cached, HEAD_SIZE), jnp.bfloat16),
            pltpu.VMEM((rows, PAIR), jnp.float32),
            pltpu.VMEM((rows, HEAD_SIZE), jnp.bfloat16),
            pltpu.VMEM((rows, HEAD_SIZE), jnp.bfloat16),
            dma((pairs + 2, 2)),
            dma((groups - 1,)),
            dma((groups,)),
            dma((2, shards, 4)),
            dma((2, shards)),
            dma((groups, pairs + 2, 3)),
            dma((groups, pairs + 2)),
        ]
        + [pltpu.VMEM((groups, 2, depth, HEAD_SIZE), jnp.bfloat16)] * (pairs + 1),
        compiler_params=pltpu.CompilerParams(
            collective_id=0, has_side_effects=True, vmem_limit_bytes=60 * 1024 * 1024
        ),
        cost_estimate=pl.CostEstimate(
            flops=2 * rows * width * (q_width + PAIR),
            bytes_accessed=depth * (q_width + PAIR) * 2,
            transcendentals=0,
        ),
        name="gather_project_attend",
    )(
        keep_flag,
        destination,
        row_counts,
        hidden,
        norm_gain.astype(jnp.float32).reshape(shards, features),
        jnp.concatenate([cosine, cosine], axis=1),
        jnp.concatenate([-sine, sine], axis=1),
        w_query,
        wk,
        wv,
        kc,
        vc,
    )


def body(
    groups,
    shards,
    hidden,
    norm_gain,
    w_query,
    key_projection_weight,
    value_projection_weight,
    prompt_key_cache,
    prompt_value_cache,
    keep_flag,
    destination,
    row_counts,
):
    return sublayer(
        shards,
        groups,
        hidden,
        norm_gain,
        w_query,
        key_projection_weight,
        value_projection_weight,
        prompt_key_cache,
        prompt_value_cache,
        keep_flag,
        destination,
        row_counts,
    )


def solution(mesh):
    return jax.shard_map(
        functools.partial(body, mesh.shape["group"], mesh.shape["fsdp"]),
        mesh=mesh,
        in_specs=(
            P("group", None, "fsdp"),
            P(),
            P("group", "fsdp"),
            P("group", None),
            P("group", None),
            P("group", None),
            P("group", None),
            P(),
            P(),
            P(),
        ),
        out_specs=P("group", None, "fsdp"),
        check_vma=False,
    )
```
